32 devices in a mesh: groups: 2 (over x), shard: 8 (over z, core), cam: 2 (over y).
Axes of the slice: x: 2, y: 2, z: 4, core: 2. Of those that a mesh axis runs over, the one named last changes fastest.
Arguments:
- params: float32 [59, 65536], P(None, ('groups', 'shard')), parts along dimension 1, as said below
- cameras: float32 [4, 4], P('groups'), parts along dimension 0, may hold values from -0.02 to 0.02
- send_rows: int32 [4, 8, 2048], P(('groups', 'cam'), 'shard'), parts along dimension 0, may hold values from 0 to 4095
- tile_ids: int32 [4, 64], P(('groups', 'cam'), 'shard'), parts along dimension 0, may hold values from 0 to 63, as said below
- tile_counts: int32 [4, 64], P(('groups', 'cam'), 'shard'), parts along dimension 0, may hold values from 0 to 512, as said below
- tile_lists: int32 [4, 64, 512], P(('groups', 'cam'), 'shard'), parts along dimension 0, may hold values from 0 to 2047, as said below
- targets: float32 [4, 64, 3, 256], P(('groups', 'cam'), 'shard'), parts along dimension 0, may hold values from 0 to 1
Outputs:
- rendered: float32 [4, 64, 3, 256], P(('groups', 'cam'), 'shard'), parts along dimension 0
- param_grad: float32 [59, 65536], P(None, ('groups', 'shard', 'cam')), parts along dimension 1
The draws below stay inside these ranges and needn't reach their ends.
There are 2 independent parts, one for each index of `groups`. The reference program is written for one: setup_inputs(seed, part) draws one part's arguments, and reference() takes and returns one part's arrays. A program takes and returns all parts, laid end to end along the dimension named above; each array names one. Nothing has to cross between parts.
Inputs may be any that keep to these rules, and one draw needn't show every extreme that they name: `params`: row 2 of every column (the centre's third coordinate) lies in 4 to 8, and row 6 (the quaternion's first entry) lies in 1 to 2. `tile_ids`: each view's row names every grid tile once. `tile_counts`: the 8 tiles of one renderer come in pairs whose counts sum to 512, one pair being 512 and 0 in every renderer, so a renderer's counts sum to 2048. `tile_lists`: entries before a tile's count name slots of its renderer that hold distinct Gaussians, in order of increasing depth (row 2 of params); over one renderer's tiles every one of its 2048 slots is named exactly once. Entries at or after the count are arbitrary slots.
All inputs are finite; a program needn't handle non-finite values.
Results may differ from the reference program's by a relative error of at most 0.0003.
Values sent between devices are 32-bit elements; how exact they have to be, the bound alone decides.
A program may use at most 128 MiB of HBM per device.

```python
import math
import jax
import jax.numpy as jnp
from jax import lax

PIX = 256
TILE_COLS = 8
G_DEV = 4096
TILES_DEV = 8
LIST = 512
RECV = 2048
CAP = 256
ALL = 64
N_SHARD = 8
N_CAM = 2


ROW_STEPS = (0, 0, 0, -1, 1, -1, -1, 1, 1)


COL_STEPS = (0, -1, 1, 0, 0, -1, 1, -1, 1)


def scene_frame(key):
    key_owner, key_depth = jax.random.split(jax.random.fold_in(key, 11))
    owner_scores = jax.random.randint(key_owner, (N_SHARD, G_DEV), 0, 1024) * G_DEV + jnp.arange(G_DEV, dtype=jnp.int32)[None, :]
    owner_order = jnp.argsort(owner_scores, axis=1).astype(jnp.int32)
    depth_rank = jax.random.permutation(key_depth, N_SHARD * G_DEV).astype(jnp.int32)
    return (owner_order, depth_rank)


def tile_layout(key):
    owner_order, depth_rank = scene_frame(key)
    key_grid, key_pairs, key_force, key_order, key_slots, key_start, key_fill = jax.random.split(jax.random.fold_in(key, 13), 7)
    per_home = G_DEV // ALL
    grid_rows = ALL // TILE_COLS
    grid_scores = jax.random.randint(key_grid, (N_CAM, ALL), 0, 1024) * ALL + jnp.arange(ALL, dtype=jnp.int32)[None, :]
    grid_tiles = jnp.argsort(grid_scores, axis=1).astype(jnp.int32)
    pair_count = TILES_DEV // 2
    first_counts = jax.random.randint(key_pairs, (N_CAM, N_SHARD, pair_count), 0, LIST + 1)
    forced = jax.random.randint(key_force, (N_CAM, N_SHARD, 1), 0, pair_count)
    first_counts = jnp.where(jnp.arange(pair_count)[None, None, :] == forced, LIST, first_counts)
    counts = jnp.concatenate([first_counts, LIST - first_counts], axis=2)
    scores = jax.random.randint(key_order, (N_CAM, N_SHARD, TILES_DEV), 0, 1024) * TILES_DEV + jnp.arange(TILES_DEV, dtype=jnp.int32)[None, None, :]
    counts = jnp.take_along_axis(counts, jnp.argsort(scores, axis=2), axis=2)
    starts = jnp.cumsum(counts, axis=2) - counts
    entry_index = jnp.arange(LIST, dtype=jnp.int32)
    used = entry_index[None, None, None, :] < counts[..., None]
    position = jnp.minimum(starts[..., None] + entry_index, RECV - 1)
    owner = position % N_SHARD
    within = position // N_SHARD
    step_in = jnp.broadcast_to(entry_index // N_SHARD, position.shape)
    grid_here = grid_tiles.reshape(N_CAM, N_SHARD, TILES_DEV)
    near_row = (grid_here // TILE_COLS)[..., None] + jnp.array(ROW_STEPS, dtype=jnp.int32)
    near_col = (grid_here % TILE_COLS)[..., None] + jnp.array(COL_STEPS, dtype=jnp.int32)
    inside = (near_row >= 0) & (near_row < grid_rows) & (near_col >= 0) & (near_col < TILE_COLS)
    near_order = jnp.argsort(jnp.where(inside, 0, 16) + jnp.arange(9, dtype=jnp.int32), axis=3)
    near_all = jnp.clip(near_row, 0, grid_rows - 1) * TILE_COLS + jnp.clip(near_col, 0, TILE_COLS - 1)
    near_tiles = jnp.take_along_axis(near_all, near_order, axis=3)
    pool = jnp.sum(inside.astype(jnp.int32), axis=3) * per_home
    start_pick = jax.random.randint(key_start, (N_CAM, N_SHARD, TILES_DEV, N_SHARD), 0, 9 * per_home)
    pick = (jnp.take_along_axis(start_pick, owner, axis=3) + step_in) % pool[..., None]
    home_tile = jnp.take_along_axis(near_tiles, pick // per_home, axis=3)
    rows = owner_order[owner, home_tile * per_home + pick % per_home]
    slot_scores = jax.random.randint(key_slots, (N_CAM, N_SHARD, N_SHARD, CAP), 0, 1024) * CAP + jnp.arange(CAP, dtype=jnp.int32)
    slot_perm = jnp.argsort(slot_scores, axis=3).astype(jnp.int32)
    view_index = jnp.arange(N_CAM, dtype=jnp.int32)[:, None, None, None]
    renderer = jnp.arange(N_SHARD, dtype=jnp.int32)[None, :, None, None]
    slot_within = slot_perm[view_index, renderer, owner, within]
    slots = owner * CAP + slot_within
    target = jnp.where(used, renderer * CAP + slot_within, RECV)
    send_rows = jnp.zeros((N_CAM, N_SHARD, RECV), jnp.int32).at[view_index, owner, target].set(rows, mode='drop')
    gaussian = owner * G_DEV + rows
    depth_key = jnp.where(used, depth_rank[gaussian], N_SHARD * G_DEV + entry_index)
    order = jnp.argsort(depth_key, axis=3)
    filler = jax.random.randint(key_fill, (N_CAM, N_SHARD, TILES_DEV, LIST), 0, RECV)
    list_slots = jnp.take_along_axis(jnp.where(used, slots, filler), order, axis=3)
    return (grid_tiles, counts.reshape(N_CAM, ALL).astype(jnp.int32), list_slots.reshape(N_CAM, ALL, LIST).astype(jnp.int32), send_rows.astype(jnp.int32))


def draw_tile_ids(key, part):
    layout = tile_layout(key)
    return layout[0]


def draw_tile_counts(key, part):
    layout = tile_layout(key)
    return layout[1]


def draw_tile_lists(key, part):
    layout = tile_layout(key)
    return layout[2]


def draw_send_rows(key, part):
    layout = tile_layout(key)
    return layout[3]


def draw_params(key, part):
    owner_order, depth_rank = scene_frame(key)
    key = jax.random.fold_in(key, 7)
    subkeys = jax.random.split(key, 13)
    gaussian_count = G_DEV * N_SHARD
    per_home = G_DEV // ALL
    grid_rows = ALL // TILE_COLS
    home = (jnp.argsort(owner_order, axis=1) // per_home).reshape(gaussian_count)
    depth_z = 4.0 + 4.0 * (depth_rank.astype(jnp.float32) + jax.random.uniform(subkeys[0], (gaussian_count,), jnp.float32)) / gaussian_count
    across = 16.0 * ((home % TILE_COLS).astype(jnp.float32) + jax.random.uniform(subkeys[1], (gaussian_count,), jnp.float32)) - 8.0 * TILE_COLS
    downward = 16.0 * ((home // TILE_COLS).astype(jnp.float32) + jax.random.uniform(subkeys[2], (gaussian_count,), jnp.float32)) - 8.0 * grid_rows
    centre = jnp.stack([across * depth_z / 1000.0, downward * depth_z / 1000.0, depth_z])
    quat_first = jax.random.uniform(subkeys[4], (1, gaussian_count), jnp.float32, 1.0, 2.0)
    solid = jax.random.uniform(subkeys[3], (1, gaussian_count), jnp.float32) < 0.006
    faint_scale = jax.random.uniform(subkeys[9], (3, gaussian_count), jnp.float32, math.log(0.02), math.log(0.12))
    solid_scale = jax.random.uniform(subkeys[10], (3, gaussian_count), jnp.float32, math.log(0.006), math.log(0.02))
    faint_logit = jax.random.uniform(subkeys[11], (1, gaussian_count), jnp.float32, -6.5, -3.0)
    solid_logit = jax.random.uniform(subkeys[12], (1, gaussian_count), jnp.float32, 5.0, 9.0)
    quat_rest = 0.6 * jax.random.normal(subkeys[5], (3, gaussian_count), jnp.float32)
    sh_base = 0.7 * jax.random.normal(subkeys[7], (3, 1, gaussian_count), jnp.float32)
    sh_high = 0.25 * jax.random.normal(subkeys[8], (3, 15, gaussian_count), jnp.float32)
    log_scale = jnp.where(solid, solid_scale, faint_scale)
    opacity_logit = jnp.where(solid, solid_logit, faint_logit)
    harmonics_coef = jnp.concatenate([sh_base, sh_high], axis=1).reshape(48, gaussian_count)
    return jnp.concatenate([centre, log_scale, quat_first, quat_rest, opacity_logit, harmonics_coef], axis=0)


def block_scale(rng, dims, cuts, least, largest):
    def one(dim, blocks):
        steps = jax.random.uniform(jax.random.fold_in(jax.random.fold_in(rng, 6), dim), (blocks,), jnp.float32, least / len(cuts), largest / len(cuts))
        return jnp.repeat(jnp.exp(steps), dims[dim] // blocks).reshape((-1,) + (1,) * (len(dims) - dim - 1))

    factor_of = one(*cuts[0])
    for cut in cuts[1:]:
        factor_of = factor_of * one(*cut)
    return factor_of


def setup_inputs(seed: int = 0, part: int = 0) -> dict:
    streams_of = jax.random.split(jax.random.key(seed), 8)
    part_keys = jax.random.split(jax.random.fold_in(streams_of[7], part), 8)
    return {
        "params": draw_params(jax.random.fold_in(jax.random.fold_in(streams_of[7], part), 71), part),
        "cameras": jnp.clip(jax.random.uniform(part_keys[1], (N_CAM, 4), jnp.float32, -0.02, 0.02), -0.02, 0.02),
        "send_rows": draw_send_rows(jax.random.fold_in(jax.random.fold_in(streams_of[7], part), 71), part),
        "tile_ids": draw_tile_ids(jax.random.fold_in(jax.random.fold_in(streams_of[7], part), 71), part),
        "tile_counts": draw_tile_counts(jax.random.fold_in(jax.random.fold_in(streams_of[7], part), 71), part),
        "tile_lists": draw_tile_lists(jax.random.fold_in(jax.random.fold_in(streams_of[7], part), 71), part),
        "targets": jnp.clip(1.0 * jax.random.uniform(part_keys[6], (N_CAM, ALL, 3, PIX), jnp.float32) ** block_scale(part_keys[6], (N_CAM, ALL, 3, PIX), ((0, 2), (1, 8)), -0.2, 0.2), 0.0, 1.0),
    }


FOCAL_LENGTH = 1000.0
SH_ZERO = 0.28209479177387814
SH_ONE = 0.4886025119029199
SH_TWO = (1.0925484305920792, -1.0925484305920792, 0.31539156525252005, -1.0925484305920792, 0.5462742152960396)
SH_THREE = (-0.5900435899266435, 2.890611442640554, -0.4570457994644658, 0.3731763325901154, -0.4570457994644658, 1.445305721320277, -0.5900435899266435)

def harmonics(dir_x, dir_y, dir_z):
    square_x = dir_x * dir_x
    square_y = dir_y * dir_y
    square_z = dir_z * dir_z
    return [jnp.full_like(dir_x, SH_ZERO), -SH_ONE * dir_y, SH_ONE * dir_z, -SH_ONE * dir_x, SH_TWO[0] * dir_x * dir_y, SH_TWO[1] * dir_y * dir_z, SH_TWO[2] * (2.0 * square_z - square_x - square_y), SH_TWO[3] * dir_x * dir_z, SH_TWO[4] * (square_x - square_y), SH_THREE[0] * dir_y * (3.0 * square_x - square_y), SH_THREE[1] * dir_x * dir_y * dir_z, SH_THREE[2] * dir_y * (4.0 * square_z - square_x - square_y), SH_THREE[3] * dir_z * (2.0 * square_z - 3.0 * square_x - 3.0 * square_y), SH_THREE[4] * dir_x * (4.0 * square_z - square_x - square_y), SH_THREE[5] * dir_z * (square_x - square_y), SH_THREE[6] * dir_x * (square_x - 3.0 * square_y)]

def project(source, camera, centre_x, centre_y):
    cosine = jnp.cos(camera[0])
    sine_angle = jnp.sin(camera[0])
    shift_x, shift_y, shift_z = (camera[1], camera[2], camera[3])
    world_x, world_y, world_z = (source[0], source[1], source[2])
    view_x = cosine * world_x - sine_angle * world_y + shift_x
    view_y = sine_angle * world_x + cosine * world_y + shift_y
    depth_z = world_z + shift_z
    inverse_z = 1.0 / depth_z
    mean_u = FOCAL_LENGTH * view_x * inverse_z + centre_x
    mean_v = FOCAL_LENGTH * view_y * inverse_z + centre_y
    scale_sq = jnp.exp(2.0 * source[3:6])
    quaternion = source[6:10] / jnp.sqrt(lax.optimization_barrier(jnp.sum(source[6:10] * source[6:10], axis=0)))
    quat_w, quat_x, quat_y, quat_z = (quaternion[0], quaternion[1], quaternion[2], quaternion[3])
    rotation = [[1.0 - 2.0 * (quat_y * quat_y + quat_z * quat_z), 2.0 * (quat_x * quat_y - quat_w * quat_z), 2.0 * (quat_x * quat_z + quat_w * quat_y)], [2.0 * (quat_x * quat_y + quat_w * quat_z), 1.0 - 2.0 * (quat_x * quat_x + quat_z * quat_z), 2.0 * (quat_y * quat_z - quat_w * quat_x)], [2.0 * (quat_x * quat_z - quat_w * quat_y), 2.0 * (quat_y * quat_z + quat_w * quat_x), 1.0 - 2.0 * (quat_x * quat_x + quat_y * quat_y)]]
    covariance = [[sum((rotation[row_axis][inner_axis] * rotation[col_axis][inner_axis] * scale_sq[inner_axis] for inner_axis in range(3))) for col_axis in range(3)] for row_axis in range(3)]
    focal_z = FOCAL_LENGTH * inverse_z
    row_first = [focal_z * cosine, -focal_z * sine_angle, -focal_z * view_x * inverse_z]
    row_second = [focal_z * sine_angle, focal_z * cosine, -focal_z * view_y * inverse_z]

    def quadratic(left_row, right_row):
        return sum((left_row[row_axis] * covariance[row_axis][col_axis] * right_row[col_axis] for row_axis in range(3) for col_axis in range(3)))
    cov_a = quadratic(row_first, row_first) + 0.3
    cov_b = quadratic(row_first, row_second)
    cov_c = quadratic(row_second, row_second) + 0.3
    determinant = cov_a * cov_c - cov_b * cov_b
    opacity = jax.nn.sigmoid(source[10])
    centre_cam_x = -(cosine * shift_x + sine_angle * shift_y)
    centre_cam_y = -(-sine_angle * shift_x + cosine * shift_y)
    centre_cam_z = -shift_z
    ray_x = world_x - centre_cam_x
    ray_y = world_y - centre_cam_y
    ray_z = world_z - centre_cam_z
    ray_length = jnp.sqrt(ray_x * ray_x + ray_y * ray_y + ray_z * ray_z)
    basis_list = harmonics(ray_x / ray_length, ray_y / ray_length, ray_z / ray_length)
    coeffs = source[11:59].reshape(3, 16, -1)
    colour = jnp.maximum(0.0, 0.5 + sum((basis_list[inner_axis] * coeffs[:, inner_axis] for inner_axis in range(16))))
    geometry = jnp.stack([mean_u, mean_v, cov_c / determinant, -cov_b / determinant, cov_a / determinant, opacity])
    return jnp.concatenate([geometry, colour], axis=0)

def pixel_grid(tile_ids):
    pixel_index = jnp.arange(PIX, dtype=jnp.int32)
    column = (tile_ids % TILE_COLS)[:, None] * 16 + pixel_index[None, :] % 16
    row_pos = (tile_ids // TILE_COLS)[:, None] * 16 + pixel_index[None, :] // 16
    return (column.astype(jnp.float32) + 0.5, row_pos.astype(jnp.float32) + 0.5)

def opacity_field(part_feats, validity, pixel_x, pixel_y):
    delta_x = pixel_x[:, None, :] - part_feats[0][:, :, None]
    delta_y = pixel_y[:, None, :] - part_feats[1][:, :, None]
    exponent = -0.5 * (part_feats[2][:, :, None] * delta_x * delta_x + part_feats[4][:, :, None] * delta_y * delta_y) - part_feats[3][:, :, None] * delta_x * delta_y
    return jnp.minimum(0.99, part_feats[5][:, :, None] * jnp.exp(exponent)) * validity[:, :, None]

def composite_full(gathered, tile_ids, tile_counts):
    pixel_x, pixel_y = pixel_grid(tile_ids)
    validity = (jnp.arange(gathered.shape[2], dtype=jnp.int32)[None, :] < tile_counts[:, None]).astype(jnp.float32)
    alpha_value = opacity_field(gathered, validity, pixel_x, pixel_y)
    log_keep = jnp.log1p(-alpha_value)
    before = jnp.cumsum(log_keep, axis=1) - log_keep
    weight = alpha_value * jnp.exp(before)
    return jnp.einsum('tnp,ctn->tcp', weight, gathered[6:9], precision=lax.Precision.HIGHEST)

def reference(params, cameras, send_rows, tile_ids, tile_counts, tile_lists, targets):
    centre_x = 8.0 * TILE_COLS
    centre_y = 8.0 * (ALL // TILE_COLS)
    owners = jnp.arange(N_SHARD, dtype=jnp.int32)
    param_grad = jnp.zeros_like(params)
    images = []
    for view_index in range(N_CAM):
        buckets = send_rows[view_index].reshape(N_SHARD, N_SHARD, CAP) + owners[:, None, None] * G_DEV
        slot_gaussian = jnp.transpose(buckets, (1, 0, 2)).reshape(N_SHARD, RECV)
        lists_view = tile_lists[view_index].reshape(N_SHARD, TILES_DEV, LIST)
        gaussian_lists = jax.vmap(jnp.take)(slot_gaussian, lists_view).astype(jnp.int32)
        ids_view = tile_ids[view_index].reshape(N_SHARD, TILES_DEV)
        counts_view = tile_counts[view_index].reshape(N_SHARD, TILES_DEV)
        camera = cameras[view_index]

        def view_image(source):
            features = project(source, camera, centre_x, centre_y)

            def one_renderer(pieces):
                return composite_full(jnp.take(features, pieces[0], axis=1), pieces[1], pieces[2])
            return lax.map(jax.checkpoint(one_renderer), (gaussian_lists, ids_view, counts_view))
        view_pixels, pull_back = jax.vjp(view_image, params)
        wanted = targets[view_index].reshape(N_SHARD, TILES_DEV, 3, PIX)
        param_grad = param_grad + pull_back((view_pixels - wanted) / PIX)[0]
        images.append(view_pixels.reshape(ALL, 3, PIX))
    return (jnp.stack(images), param_grad)
```

```python
import functools

import jax
import jax.numpy as jnp
import numpy as np
from jax import lax
from jax.experimental import pallas as pl
from jax.experimental.pallas import tpu as pltpu
from jax.sharding import PartitionSpec as P

PIX = 256
TILE_COLS = 8
LANES = 128
FEATS = 9
ROWS = 16
CLAMP = 0.99
FOCAL_LENGTH = 1000.0
SH_ZERO = 0.28209479177387814
SH_ONE = 0.4886025119029199
SH_TWO = (
    1.0925484305920792,
    -1.0925484305920792,
    0.31539156525252005,
    -1.0925484305920792,
    0.5462742152960396,
)
SH_THREE = (
    -0.5900435899266435,
    2.890611442640554,
    -0.4570457994644658,
    0.3731763325901154,
    -0.4570457994644658,
    1.445305721320277,
    -0.5900435899266435,
)
F32 = jnp.float32
BF16 = jnp.bfloat16
NT = (((1,), (1,)), ((), ()))
VMEM_LIMIT = 48 * 1024 * 1024


def unit_like(value):
    if isinstance(value, Pair):
        return Pair(jnp.ones_like(value.high), jnp.zeros_like(value.low))
    return jnp.ones_like(value)


def harmonics(dir_x, dir_y, dir_z):
    square_x = dir_x * dir_x
    square_y = dir_y * dir_y
    square_z = dir_z * dir_z
    return [
        unit_like(dir_x) * SH_ZERO,
        -SH_ONE * dir_y,
        SH_ONE * dir_z,
        -SH_ONE * dir_x,
        SH_TWO[0] * dir_x * dir_y,
        SH_TWO[1] * dir_y * dir_z,
        SH_TWO[2] * (2.0 * square_z - square_x - square_y),
        SH_TWO[3] * dir_x * dir_z,
        SH_TWO[4] * (square_x - square_y),
        SH_THREE[0] * dir_y * (3.0 * square_x - square_y),
        SH_THREE[1] * dir_x * dir_y * dir_z,
        SH_THREE[2] * dir_y * (4.0 * square_z - square_x - square_y),
        SH_THREE[3] * dir_z * (2.0 * square_z - 3.0 * square_x - 3.0 * square_y),
        SH_THREE[4] * dir_x * (4.0 * square_z - square_x - square_y),
        SH_THREE[5] * dir_z * (square_x - square_y),
        SH_THREE[6] * dir_x * (square_x - 3.0 * square_y),
    ]


def camera_of(cam_ref, view):
    angle = jnp.full((1, LANES), cam_ref[view, 0], F32)
    return (jnp.cos(angle), jnp.sin(angle), cam_ref[view, 1], cam_ref[view, 2], cam_ref[view, 3])


def geometry(camera, centre, source):
    cosine, sine, shift_x, shift_y, shift_z = camera
    world_x, world_y, world_z = source[0:3]
    view_x = cosine * world_x - sine * world_y + shift_x
    view_y = sine * world_x + cosine * world_y + shift_y
    inverse_z = 1.0 / (world_z + shift_z)
    mean_u = FOCAL_LENGTH * view_x * inverse_z + centre[0]
    mean_v = FOCAL_LENGTH * view_y * inverse_z + centre[1]
    scale_sq = [jnp.exp(2.0 * value) for value in source[3:6]]
    norm = lax.rsqrt(sum(value * value for value in source[6:10]))
    quat_w, quat_x, quat_y, quat_z = [value * norm for value in source[6:10]]
    rotation = [
        [
            1.0 - 2.0 * (quat_y * quat_y + quat_z * quat_z),
            2.0 * (quat_x * quat_y - quat_w * quat_z),
            2.0 * (quat_x * quat_z + quat_w * quat_y),
        ],
        [
            2.0 * (quat_x * quat_y + quat_w * quat_z),
            1.0 - 2.0 * (quat_x * quat_x + quat_z * quat_z),
            2.0 * (quat_y * quat_z - quat_w * quat_x),
        ],
        [
            2.0 * (quat_x * quat_z - quat_w * quat_y),
            2.0 * (quat_y * quat_z + quat_w * quat_x),
            1.0 - 2.0 * (quat_x * quat_x + quat_y * quat_y),
        ],
    ]
    focal_z = FOCAL_LENGTH * inverse_z
    first = [focal_z * cosine, -focal_z * sine, -focal_z * view_x * inverse_z]
    second = [focal_z * sine, focal_z * cosine, -focal_z * view_y * inverse_z]
    first_q = [sum(first[i] * rotation[i][k] for i in range(3)) for k in range(3)]
    second_q = [sum(second[i] * rotation[i][k] for i in range(3)) for k in range(3)]
    cov_a = sum(first_q[k] * first_q[k] * scale_sq[k] for k in range(3)) + 0.3
    cov_b = sum(first_q[k] * second_q[k] * scale_sq[k] for k in range(3))
    cov_c = sum(second_q[k] * second_q[k] * scale_sq[k] for k in range(3)) + 0.3
    inverse_det = 1.0 / (cov_a * cov_c - cov_b * cov_b)
    return [mean_u, mean_v, cov_c * inverse_det, -cov_b * inverse_det, cov_a * inverse_det]


def basis_of(camera, world):
    cosine, sine, shift_x, shift_y, shift_z = camera
    ray_x = world[0] + (cosine * shift_x + sine * shift_y)
    ray_y = world[1] + (-sine * shift_x + cosine * shift_y)
    ray_z = world[2] + shift_z
    inverse = lax.rsqrt(ray_x * ray_x + ray_y * ray_y + ray_z * ray_z)
    return harmonics(ray_x * inverse, ray_y * inverse, ray_z * inverse)


def two_sum(a, b):
    total = a + b
    part = total - a
    return total, (a - (total - part)) + (b - part)


def two_prod(a, b):
    total = a * b
    wide_a, wide_b = 4097.0 * a, 4097.0 * b
    a_high = wide_a - (wide_a - a)
    b_high = wide_b - (wide_b - b)
    a_low, b_low = a - a_high, b - b_high
    error = ((a_high * b_high - total) + a_high * b_low + a_low * b_high) + a_low * b_low
    return total, error


class Pair:
    def __init__(self, high, low):
        self.high, self.low = high, low

    def __add__(self, other):
        if not isinstance(other, Pair):
            other = Pair(other, 0.0)
        total, error = two_sum(self.high, other.high)
        return Pair(*two_sum(total, error + (self.low + other.low)))

    __radd__ = __add__

    def __neg__(self):
        return Pair(-self.high, -self.low)

    def __sub__(self, other):
        return self + (-other)

    def __mul__(self, other):
        if not isinstance(other, Pair):
            if isinstance(other, float):
                high = float(np.float32(other))
                other = Pair(jnp.full_like(self.high, high), other - high)
            else:
                other = Pair(other, 0.0)
        total, error = two_prod(self.high, other.high)
        return Pair(*two_sum(total, error + (self.high * other.low + self.low * other.high)))

    __rmul__ = __mul__


def colour_totals(camera, world, par_ref):
    cosine, sine, shift_x, shift_y, shift_z = camera
    plain = basis_of(camera, world)
    zero = jnp.zeros_like(world[0])
    first = cosine * shift_x + sine * shift_y
    second = -sine * shift_x + cosine * shift_y
    ray = [Pair(*two_sum(world[0], zero + first)), Pair(*two_sum(world[1], zero + second))]
    ray.append(Pair(*two_sum(world[2], zero + shift_z)))
    square = ray[0] * ray[0] + ray[1] * ray[1] + ray[2] * ray[2]
    guess = lax.rsqrt(square.high)
    rest = (square * guess) * guess + (zero - 1.0)
    inverse = Pair(*two_sum(guess, -0.5 * guess * (rest.high + rest.low)))
    direction = [value * inverse for value in ray]
    basis = harmonics(*direction)
    totals = []
    for channel in range(3):
        coeffs = [par_ref[11 + 16 * channel + k] for k in range(16)]
        total = Pair(zero + 0.5, zero)
        for k in range(16):
            total = total + basis[k] * coeffs[k]
        careful = total.high + total.low
        simple = 0.5 + sum(plain[k] * coeffs[k] for k in range(16))
        totals.append(jnp.where(careful - careful == 0.0, careful, simple))
    return totals


def pieces_of(value, count):
    parts = []
    for _ in range(count - 1):
        part = value.astype(BF16).astype(F32)
        parts.append(part)
        value = value - part
    parts.append(value)
    return parts


def split_pair(value):
    high = value.astype(BF16)
    return high, (value - high.astype(F32)).astype(BF16)


def one_hot(rows, index):
    grid = lax.broadcasted_iota(jnp.int32, (rows, index.shape[1]), 0)
    return grid == index


def as_bf16(mask):
    return jnp.where(mask, 1.0, 0.0).astype(BF16)


def peers_of(axis, count):
    me = lax.axis_index(axis)
    return me, [lax.rem(me + step, count) for step in range(1, count)]


def greet(groups):
    barrier = pltpu.get_barrier_semaphore()
    for axis, partners in groups:
        for partner in partners:
            pl.semaphore_signal(
                barrier, inc=1, device_id={axis: partner}, device_id_type=pl.DeviceIdType.MESH
            )
    pl.semaphore_wait(barrier, sum(len(partners) for _, partners in groups))


def push(axis, partner, source, target, send_sem, recv_sem):
    return pltpu.make_async_remote_copy(
        src_ref=source,
        dst_ref=target,
        send_sem=send_sem,
        recv_sem=recv_sem,
        device_id={axis: partner},
        device_id_type=pl.DeviceIdType.MESH,
    )


def project_kernel(centre, cam_ref, par_ref, table_ref, gate_ref):
    camera = camera_of(cam_ref, lax.axis_index("cam"))
    groups = par_ref.shape[1]
    source = [par_ref[k] for k in range(10)]
    feats = geometry(camera, centre, source)
    feats.append(1.0 / (1.0 + jnp.exp(-par_ref[10])))
    for channel, total in enumerate(colour_totals(camera, source[0:3], par_ref)):
        feats.append(jnp.maximum(0.0, total))
        gate_ref[channel] = jnp.where(total > 0.0, 1.0, jnp.where(total == 0.0, 0.5, 0.0))
    for f in range(FEATS):
        for piece, value in enumerate(pieces_of(feats[f], 3)):
            table_ref[pl.ds((f * 3 + piece) * groups, groups), :] = value.astype(BF16)


def send_kernel(shards, table, rows_ref, out_ref, staged, landed, send_sem, recv_sem):
    me, partners = peers_of("shard", shards)
    greet([("shard", partners)])
    groups = table.shape[0] // (3 * FEATS)
    cap = out_ref.shape[2]

    def gathered(r):
        index = rows_ref[pl.ds(r, 1), :]
        low = as_bf16(one_hot(LANES, index & (LANES - 1)))
        high = one_hot(groups, lax.shift_right_logical(index, 7))
        found = jnp.dot(table[...], low, preferred_element_type=F32)
        values = []
        for f in range(FEATS):
            base = f * 3 * groups
            value = (
                found[base : base + groups]
                + found[base + groups : base + 2 * groups]
                + found[base + 2 * groups : base + 3 * groups]
            )
            values.append(jnp.sum(jnp.where(high, value, 0.0), axis=0, keepdims=True))
        return stack_rows(values, ROWS)

    copies = []
    for step, partner in enumerate(partners):
        staged[step] = gathered(partner)
        copy = push(
            "shard",
            partner,
            staged.at[step],
            landed.at[step],
            send_sem.at[step],
            recv_sem.at[step],
        )
        copy.start()
        copies.append(copy)
    out_ref[me] = gathered(me)
    for step, copy in enumerate(copies):
        copy.wait_recv()
        out_ref[lax.rem(me + (shards - 1 - step), shards)] = landed[step]
    for copy in copies:
        copy.wait_send()


def stack_rows(values, rows):
    row = lax.broadcasted_iota(jnp.int32, (rows, values[0].shape[1]), 0)
    out = jnp.zeros(row.shape, F32)
    for k, value in enumerate(values):
        out = jnp.where(row == k, value, out)
    return out


def mono_value(kind, x, y):
    return jnp.where(
        kind == 0,
        1.0,
        jnp.where(
            kind == 1,
            x,
            jnp.where(
                kind == 2,
                y,
                jnp.where(
                    kind == 3,
                    x * x,
                    jnp.where(kind == 4, x * y, jnp.where(kind == 5, y * y, 0.0)),
                ),
            ),
        ),
    )


def pixel_offset(index):
    return (index & 15).astype(F32) - 7.5, lax.shift_right_logical(index, 4).astype(F32) - 7.5


def render_kernel(
    tiles,
    blocks,
    ids_ref,
    counts_ref,
    feats_ref,
    lists_ref,
    wanted_ref,
    image_ref,
    grad_ref,
    table,
    mono_row,
    upper,
    lower,
    keep_x,
    keep_wh,
    keep_wl,
    keep_f,
    carry,
    image,
    acc,
):
    shards, _, cap = feats_ref.shape
    per = cap // LANES
    groups = shards * per
    for h in range(groups):
        s, part = h // per, h % per
        block = feats_ref[s, :, part * LANES : (part + 1) * LANES]
        table[pl.ds(h * 48, 48), :] = jnp.concatenate(pieces_of(block, 3), axis=0).astype(BF16)
    k = lax.broadcasted_iota(jnp.int32, (ROWS, PIX), 0)
    x, y = pixel_offset(lax.broadcasted_iota(jnp.int32, (ROWS, PIX), 1))
    mono_row[...] = mono_value(k, x, y).astype(BF16)
    n = lax.broadcasted_iota(jnp.int32, (LANES, 2 * LANES), 0)
    m = lax.broadcasted_iota(jnp.int32, (LANES, 2 * LANES), 1)
    upper[...] = as_bf16((n < m) | (m >= LANES))
    lower[...] = as_bf16((n > m) | (m >= LANES))
    acc[...] = jnp.zeros_like(acc)
    lane = lax.broadcasted_iota(jnp.int32, (1, LANES), 1)

    def one_tile(t, _):
        count = counts_ref[0, t]
        grid_id = ids_ref[0, t]
        origin_x = (16 * lax.rem(grid_id, TILE_COLS) + 8).astype(F32)
        origin_y = (16 * lax.div(grid_id, TILE_COLS) + 8).astype(F32)
        steps = lax.div(count + (LANES - 1), LANES)
        carry[...] = jnp.zeros_like(carry)
        image[...] = jnp.zeros_like(image)

        def entry_index(j):
            return lists_ref[pl.ds(t * blocks + j, 1), :]

        def forward(j, _):
            index = entry_index(j)
            low = as_bf16(one_hot(LANES, index & (LANES - 1)))
            high = lax.shift_right_logical(index, 7)
            found = jnp.dot(table[...], low, preferred_element_type=F32)
            total = jnp.zeros((48, LANES), F32)
            for h in range(groups):
                total = total + jnp.where(high == h, found[h * 48 : (h + 1) * 48], 0.0)
            feats = total[0:16] + total[16:32] + total[32:48]
            keep_f[j] = feats
            ux = feats[0:1] - origin_x
            uy = feats[1:2] - origin_y
            c0, c1, c2 = feats[2:3], feats[3:4], feats[4:5]
            valid = j * LANES + lane < count
            offset = lax.broadcasted_iota(jnp.int32, (16, LANES), 0).astype(F32) - 7.5
            dx = offset - ux
            dy = offset - uy
            along_x = jnp.where(valid, -0.5 * c0 * dx * dx, 0.0)
            cross = jnp.where(valid, -c1 * dx, 0.0)
            along_y = jnp.where(valid, -0.5 * c2 * dy * dy, -1e30)
            value = feats[5:6] * jnp.exp(
                jnp.concatenate(
                    [
                        (along_x + along_y[r : r + 1]) + cross * dy[r : r + 1]
                        for r in range(PIX // 16)
                    ],
                    axis=0,
                )
            )
            keep_x[j] = value
            alpha = jnp.minimum(CLAMP, value)
            log_high, log_low = split_pair(jnp.log(1.0 - alpha))
            before = jnp.dot(log_high, upper[...], preferred_element_type=F32) + jnp.dot(
                log_low, upper[...], preferred_element_type=F32
            )
            held = carry[...]
            weight = alpha * jnp.exp(before[:, :LANES] + held)
            carry[...] = held + before[:, LANES:]
            w_high, w_low = split_pair(weight)
            keep_wh[j] = w_high
            keep_wl[j] = w_low
            colour = stack_rows([feats[6:7], feats[7:8], feats[8:9]], 8)
            colour = jnp.concatenate(pieces_of(colour, 2), axis=0).astype(BF16)
            drawn = lax.dot_general(colour, w_high, NT, preferred_element_type=F32)
            drawn = drawn + lax.dot_general(colour, w_low, NT, preferred_element_type=F32)
            image[...] += drawn[0:8] + drawn[8:16]
            return 0

        lax.fori_loop(0, steps, forward, 0)
        shown = image[0:3]
        image_ref[t] = shown
        slope = (shown - wanted_ref[t]) * (1.0 / PIX)
        slope = stack_rows([slope[0:1], slope[1:2], slope[2:3]], 8)
        g_high, g_low = pieces_of(slope, 2)
        g_row = jnp.concatenate([g_high, g_low], axis=0).astype(BF16)
        g_col = jnp.transpose(jnp.concatenate([g_high, g_high, g_low, g_low], axis=0)).astype(BF16)
        carry[...] = jnp.zeros_like(carry)

        def backward(step, _):
            j = steps - 1 - step
            feats = keep_f[j]
            colour = stack_rows([feats[6:7], feats[7:8], feats[8:9]], 8)
            c_high, c_low = pieces_of(colour, 2)
            colour = jnp.concatenate([c_high, c_low, c_high, c_low], axis=0).astype(BF16)
            pull = jnp.dot(g_col, colour, preferred_element_type=F32)
            w_high, w_low = keep_wh[j], keep_wl[j]
            share = (w_high.astype(F32) + w_low.astype(F32)) * pull
            s_high, s_low = split_pair(share)
            after = jnp.dot(s_high, lower[...], preferred_element_type=F32) + jnp.dot(
                s_low, lower[...], preferred_element_type=F32
            )
            held = carry[...]
            behind = after[:, :LANES] + held
            carry[...] = held + after[:, LANES:]
            value = keep_x[j]
            free = value < CLAMP
            odds = value / (1.0 - jnp.minimum(value, CLAMP))
            p_high, p_low = split_pair(jnp.where(free, share - odds * behind, 0.0))
            mom = jnp.dot(mono_row[...], p_high, preferred_element_type=F32) + jnp.dot(
                mono_row[...], p_low, preferred_element_type=F32
            )
            tint = jnp.dot(g_row, w_high, preferred_element_type=F32) + jnp.dot(
                g_row, w_low, preferred_element_type=F32
            )
            tint = tint[0:8] + tint[8:16]
            ux = feats[0:1] - origin_x
            uy = feats[1:2] - origin_y
            c0, c1, c2 = feats[2:3], feats[3:4], feats[4:5]
            m0, mx, my = mom[0:1], mom[1:2], mom[2:3]
            px = mx - ux * m0
            py = my - uy * m0
            pxx = mom[3:4] - ux * (mx + px)
            pxy = mom[4:5] - ux * my - uy * px
            pyy = mom[5:6] - uy * (my + py)
            grads = stack_rows(
                [
                    c0 * px + c1 * py,
                    c2 * py + c1 * px,
                    -0.5 * pxx,
                    -pxy,
                    -0.5 * pyy,
                    m0,
                    tint[0:1],
                    tint[1:2],
                    tint[2:3],
                ],
                ROWS,
            )
            grads = jnp.concatenate(pieces_of(grads, 2), axis=0)
            index = entry_index(j)
            low = as_bf16(one_hot(LANES, index & (LANES - 1)))
            high = lax.shift_right_logical(index, 7)
            valid = j * LANES + lane < count
            grads = jnp.where(valid, grads, 0.0)
            spread = jnp.concatenate(
                [jnp.where(high == h, grads, 0.0) for h in range(groups)], axis=0
            ).astype(BF16)
            acc[...] += lax.dot_general(spread, low, NT, preferred_element_type=F32)
            return 0

        lax.fori_loop(0, steps, backward, 0)
        return 0

    lax.fori_loop(0, tiles, one_tile, 0)
    for h in range(groups):
        s, part = h // per, h % per
        grad_ref[s, :, part * LANES : (part + 1) * LANES] = (
            acc[pl.ds(h * 32, 16), :] + acc[pl.ds(h * 32 + 16, 16), :]
        )


def return_kernel(
    shards,
    cams,
    centre,
    cam_ref,
    par_ref,
    slot_ref,
    rows_ref,
    gate_ref,
    out_ref,
    acc,
    landed,
    mine,
    other,
    shard_send,
    shard_recv,
    cam_send,
    cam_recv,
):
    me, partners = peers_of("shard", shards)
    here, views = peers_of("cam", cams)
    greet([("shard", partners), ("cam", views)])
    size = out_ref.shape[1]
    groups = cams * size
    copies = []
    for step, partner in enumerate(partners):
        copy = push(
            "shard",
            partner,
            slot_ref.at[partner],
            landed.at[step],
            shard_send.at[step],
            shard_recv.at[step],
        )
        copy.start()
        copies.append(copy)

    def scattered(r, value):
        index = rows_ref[pl.ds(r, 1), :]
        low = as_bf16(one_hot(LANES, index & (LANES - 1)))
        high = one_hot(groups, lax.shift_right_logical(index, 7))
        parts = pieces_of(value, 2)
        spread = jnp.concatenate(
            [
                jnp.where(high, part[f : f + 1], 0.0).astype(BF16)
                for f in range(FEATS)
                for part in parts
            ],
            axis=0,
        )
        return lax.dot_general(spread, low, NT, preferred_element_type=F32)

    acc[...] = scattered(me, slot_ref[me])
    for step, copy in enumerate(copies):
        copy.wait_recv()
        acc[...] += scattered(lax.rem(me + (shards - 1 - step), shards), landed[step])
    for f in range(FEATS):
        value = acc[pl.ds(2 * f * groups, groups), :] + acc[pl.ds((2 * f + 1) * groups, groups), :]
        if f >= 6:
            value = value * gate_ref[f - 6]
        for c in range(cams):
            mine[c, f] = value[c * size : (c + 1) * size]
    swaps = []
    for step, view in enumerate(views):
        copy = push(
            "cam", view, mine.at[view], other.at[step], cam_send.at[step], cam_recv.at[step]
        )
        copy.start()
        swaps.append(copy)
    source = [par_ref[k] for k in range(10)]
    keep = 1.0 / (1.0 + jnp.exp(par_ref[10]))

    def one_view(view, feature_grad, first):
        camera = camera_of(cam_ref, view)
        _, pull_geometry = jax.vjp(lambda *s: geometry(camera, centre, s), *source)
        head = list(pull_geometry([feature_grad(f) for f in range(5)]))
        basis, pull_basis = jax.vjp(lambda *w: basis_of(camera, w), *source[0:3])
        tints = [feature_grad(6 + channel) for channel in range(3)]
        cotangent = [
            sum(tints[channel] * par_ref[11 + 16 * channel + k] for channel in range(3))
            for k in range(16)
        ]
        for k, value in enumerate(pull_basis(cotangent)):
            head[k] = head[k] + value

        def put(k, value):
            if first:
                out_ref[k] = value
            else:
                out_ref[k] += value

        for k in range(10):
            put(k, head[k])
        put(10, keep * feature_grad(5))
        for channel in range(3):
            for k in range(16):
                put(11 + 16 * channel + k, tints[channel] * basis[k])

    one_view(here, lambda f: mine[here, f], True)
    for step, copy in enumerate(swaps):
        copy.wait_recv()
        one_view(
            lax.rem(here + (cams - 1 - step), cams), lambda f, step=step: other[step, f], False
        )
    for copy in copies + swaps:
        copy.wait_send()


def local_params():
    return pltpu.CompilerParams(vmem_limit_bytes=VMEM_LIMIT)


def remote_params(number):
    return pltpu.CompilerParams(
        vmem_limit_bytes=VMEM_LIMIT, collective_id=number, has_side_effects=True
    )


VM = pl.BlockSpec(memory_space=pltpu.VMEM)
SM = pl.BlockSpec(memory_space=pltpu.SMEM)


def per_device(params, cameras, send_rows, tile_ids, tile_counts, tile_lists, targets):
    shards = lax.axis_size("shard")
    cams = lax.axis_size("cam")
    tiles, length = tile_lists.shape[1:]
    blocks = length // LANES
    centre = (8.0 * TILE_COLS, 8.0 * (shards * tiles // TILE_COLS))
    slots = send_rows.shape[2]
    cap = slots // shards
    groups = params.shape[1] // LANES
    size = groups // cams
    wide = params.reshape(params.shape[0], groups, LANES)
    rows = send_rows.reshape(shards, cap)
    table, gates = pl.pallas_call(
        functools.partial(project_kernel, centre),
        out_shape=(
            jax.ShapeDtypeStruct((3 * FEATS * groups, LANES), BF16),
            jax.ShapeDtypeStruct((3, groups, LANES), F32),
        ),
        in_specs=[SM, VM],
        out_specs=(VM, VM),
        compiler_params=local_params(),
        name="project",
    )(cameras, wide)
    links = pltpu.SemaphoreType.DMA((shards - 1,))
    arrived = pl.pallas_call(
        functools.partial(send_kernel, shards),
        out_shape=jax.ShapeDtypeStruct((shards, ROWS, cap), F32),
        in_specs=[VM, VM],
        out_specs=VM,
        scratch_shapes=[
            pltpu.VMEM((shards - 1, ROWS, cap), F32),
            pltpu.VMEM((shards - 1, ROWS, cap), F32),
            links,
            links,
        ],
        compiler_params=remote_params(0),
        name="send",
    )(table, rows)
    image, slot_grad = pl.pallas_call(
        functools.partial(render_kernel, tiles, blocks),
        out_shape=(
            jax.ShapeDtypeStruct((tiles, 3, PIX), F32),
            jax.ShapeDtypeStruct((shards, ROWS, cap), F32),
        ),
        in_specs=[SM, SM, VM, VM, VM],
        out_specs=(VM, VM),
        scratch_shapes=[
            pltpu.VMEM((slots // LANES * 48, LANES), BF16),
            pltpu.VMEM((ROWS, PIX), BF16),
            pltpu.VMEM((LANES, 2 * LANES), BF16),
            pltpu.VMEM((LANES, 2 * LANES), BF16),
            pltpu.VMEM((blocks, PIX, LANES), F32),
            pltpu.VMEM((blocks, PIX, LANES), BF16),
            pltpu.VMEM((blocks, PIX, LANES), BF16),
            pltpu.VMEM((blocks, ROWS, LANES), F32),
            pltpu.VMEM((PIX, LANES), F32),
            pltpu.VMEM((8, PIX), F32),
            pltpu.VMEM((slots // LANES * 32, LANES), F32),
        ],
        compiler_params=local_params(),
        name="render",
    )(
        tile_ids,
        tile_counts,
        arrived,
        tile_lists[0].reshape(tiles * blocks, LANES),
        targets[0],
    )
    mine = lax.dynamic_slice_in_dim(wide, lax.axis_index("cam") * size, size, axis=1)
    grad = pl.pallas_call(
        functools.partial(return_kernel, shards, cams, centre),
        out_shape=jax.ShapeDtypeStruct((params.shape[0], size, LANES), F32),
        in_specs=[SM, VM, VM, VM, VM],
        out_specs=VM,
        scratch_shapes=[
            pltpu.VMEM((2 * FEATS * groups, LANES), F32),
            pltpu.VMEM((shards - 1, ROWS, cap), F32),
            pltpu.VMEM((cams, FEATS, size, LANES), F32),
            pltpu.VMEM((cams - 1, FEATS, size, LANES), F32),
            links,
            links,
            pltpu.SemaphoreType.DMA((cams - 1,)),
            pltpu.SemaphoreType.DMA((cams - 1,)),
        ],
        compiler_params=remote_params(1),
        name="return_pull",
    )(cameras, mine, slot_grad, rows, gates)
    return (image[None], grad.reshape(params.shape[0], size * LANES))


def solution(mesh):
    placed = (
        P(None, ("groups", "shard")),
        P("groups", None),
        P(("groups", "cam"), "shard", None),
        P(("groups", "cam"), "shard"),
        P(("groups", "cam"), "shard"),
        P(("groups", "cam"), "shard", None),
        P(("groups", "cam"), "shard", None, None),
    )
    return jax.shard_map(
        per_device,
        mesh=mesh,
        in_specs=placed,
        out_specs=(P(("groups", "cam"), "shard", None, None), P(None, ("groups", "shard", "cam"))),
        check_vma=False,
    )
```

```python
import functools

import jax
import jax.numpy as jnp
import numpy as np
from jax import lax
from jax.experimental import pallas as pl
from jax.experimental.pallas import tpu as pltpu
from jax.sharding import PartitionSpec as P

PIX = 256
TILE_COLS = 8
LANES = 128
BLOCK = 256
FEATS = 9
ROWS = 16
CLAMP = 0.99
FOCAL_LENGTH = 1000.0
SH_ZERO = 0.28209479177387814
SH_ONE = 0.4886025119029199
SH_TWO = (
    1.0925484305920792,
    -1.0925484305920792,
    0.31539156525252005,
    -1.0925484305920792,
    0.5462742152960396,
)
SH_THREE = (
    -0.5900435899266435,
    2.890611442640554,
    -0.4570457994644658,
    0.3731763325901154,
    -0.4570457994644658,
    1.445305721320277,
    -0.5900435899266435,
)
F32 = jnp.float32
BF16 = jnp.bfloat16
NT = (((1,), (1,)), ((), ()))
VMEM_LIMIT = 48 * 1024 * 1024


def unit_like(value):
    if isinstance(value, Pair):
        return Pair(jnp.ones_like(value.high), jnp.zeros_like(value.low))
    return jnp.ones_like(value)


def harmonics(dir_x, dir_y, dir_z):
    square_x = dir_x * dir_x
    square_y = dir_y * dir_y
    square_z = dir_z * dir_z
    return [
        unit_like(dir_x) * SH_ZERO,
        -SH_ONE * dir_y,
        SH_ONE * dir_z,
        -SH_ONE * dir_x,
        SH_TWO[0] * dir_x * dir_y,
        SH_TWO[1] * dir_y * dir_z,
        SH_TWO[2] * (2.0 * square_z - square_x - square_y),
        SH_TWO[3] * dir_x * dir_z,
        SH_TWO[4] * (square_x - square_y),
        SH_THREE[0] * dir_y * (3.0 * square_x - square_y),
        SH_THREE[1] * dir_x * dir_y * dir_z,
        SH_THREE[2] * dir_y * (4.0 * square_z - square_x - square_y),
        SH_THREE[3] * dir_z * (2.0 * square_z - 3.0 * square_x - 3.0 * square_y),
        SH_THREE[4] * dir_x * (4.0 * square_z - square_x - square_y),
        SH_THREE[5] * dir_z * (square_x - square_y),
        SH_THREE[6] * dir_x * (square_x - 3.0 * square_y),
    ]


def camera_of(cam_ref, view):
    angle = jnp.full((1, LANES), cam_ref[view, 0], F32)
    return (jnp.cos(angle), jnp.sin(angle), cam_ref[view, 1], cam_ref[view, 2], cam_ref[view, 3])


def geometry(camera, centre, source):
    cosine, sine, shift_x, shift_y, shift_z = camera
    world_x, world_y, world_z = source[0:3]
    view_x = cosine * world_x - sine * world_y + shift_x
    view_y = sine * world_x + cosine * world_y + shift_y
    inverse_z = 1.0 / (world_z + shift_z)
    mean_u = FOCAL_LENGTH * view_x * inverse_z + centre[0]
    mean_v = FOCAL_LENGTH * view_y * inverse_z + centre[1]
    scale_sq = [jnp.exp(2.0 * value) for value in source[3:6]]
    norm = lax.rsqrt(sum(value * value for value in source[6:10]))
    quat_w, quat_x, quat_y, quat_z = [value * norm for value in source[6:10]]
    rotation = [
        [
            1.0 - 2.0 * (quat_y * quat_y + quat_z * quat_z),
            2.0 * (quat_x * quat_y - quat_w * quat_z),
            2.0 * (quat_x * quat_z + quat_w * quat_y),
        ],
        [
            2.0 * (quat_x * quat_y + quat_w * quat_z),
            1.0 - 2.0 * (quat_x * quat_x + quat_z * quat_z),
            2.0 * (quat_y * quat_z - quat_w * quat_x),
        ],
        [
            2.0 * (quat_x * quat_z - quat_w * quat_y),
            2.0 * (quat_y * quat_z + quat_w * quat_x),
            1.0 - 2.0 * (quat_x * quat_x + quat_y * quat_y),
        ],
    ]
    focal_z = FOCAL_LENGTH * inverse_z
    first = [focal_z * cosine, -focal_z * sine, -focal_z * view_x * inverse_z]
    second = [focal_z * sine, focal_z * cosine, -focal_z * view_y * inverse_z]
    first_q = [sum(first[i] * rotation[i][k] for i in range(3)) for k in range(3)]
    second_q = [sum(second[i] * rotation[i][k] for i in range(3)) for k in range(3)]
    cov_a = sum(first_q[k] * first_q[k] * scale_sq[k] for k in range(3)) + 0.3
    cov_b = sum(first_q[k] * second_q[k] * scale_sq[k] for k in range(3))
    cov_c = sum(second_q[k] * second_q[k] * scale_sq[k] for k in range(3)) + 0.3
    inverse_det = 1.0 / (cov_a * cov_c - cov_b * cov_b)
    return [mean_u, mean_v, cov_c * inverse_det, -cov_b * inverse_det, cov_a * inverse_det]


def basis_of(camera, world):
    cosine, sine, shift_x, shift_y, shift_z = camera
    ray_x = world[0] + (cosine * shift_x + sine * shift_y)
    ray_y = world[1] + (-sine * shift_x + cosine * shift_y)
    ray_z = world[2] + shift_z
    inverse = lax.rsqrt(ray_x * ray_x + ray_y * ray_y + ray_z * ray_z)
    return harmonics(ray_x * inverse, ray_y * inverse, ray_z * inverse)


def two_sum(a, b):
    total = a + b
    part = total - a
    return total, (a - (total - part)) + (b - part)


def two_prod(a, b):
    total = a * b
    wide_a, wide_b = 4097.0 * a, 4097.0 * b
    a_high = wide_a - (wide_a - a)
    b_high = wide_b - (wide_b - b)
    a_low, b_low = a - a_high, b - b_high
    error = ((a_high * b_high - total) + a_high * b_low + a_low * b_high) + a_low * b_low
    return total, error


class Pair:
    def __init__(self, high, low):
        self.high, self.low = high, low

    def __add__(self, other):
        if not isinstance(other, Pair):
            other = Pair(other, 0.0)
        total, error = two_sum(self.high, other.high)
        return Pair(*two_sum(total, error + (self.low + other.low)))

    __radd__ = __add__

    def __neg__(self):
        return Pair(-self.high, -self.low)

    def __sub__(self, other):
        return self + (-other)

    def __mul__(self, other):
        if not isinstance(other, Pair):
            if isinstance(other, float):
                high = float(np.float32(other))
                other = Pair(jnp.full_like(self.high, high), other - high)
            else:
                other = Pair(other, 0.0)
        total, error = two_prod(self.high, other.high)
        return Pair(*two_sum(total, error + (self.high * other.low + self.low * other.high)))

    __rmul__ = __mul__


def colour_totals(camera, world, par_ref):
    cosine, sine, shift_x, shift_y, shift_z = camera
    plain = basis_of(camera, world)
    zero = jnp.zeros_like(world[0])
    first = cosine * shift_x + sine * shift_y
    second = -sine * shift_x + cosine * shift_y
    ray = [Pair(*two_sum(world[0], zero + first)), Pair(*two_sum(world[1], zero + second))]
    ray.append(Pair(*two_sum(world[2], zero + shift_z)))
    square = ray[0] * ray[0] + ray[1] * ray[1] + ray[2] * ray[2]
    guess = lax.rsqrt(square.high)
    rest = (square * guess) * guess + (zero - 1.0)
    inverse = Pair(*two_sum(guess, -0.5 * guess * (rest.high + rest.low)))
    direction = [value * inverse for value in ray]
    basis = harmonics(*direction)
    totals = []
    for channel in range(3):
        coeffs = [par_ref[11 + 16 * channel + k] for k in range(16)]
        total = Pair(zero + 0.5, zero)
        for k in range(16):
            total = total + basis[k] * coeffs[k]
        careful = total.high + total.low
        simple = 0.5 + sum(plain[k] * coeffs[k] for k in range(16))
        totals.append(jnp.where(careful - careful == 0.0, careful, simple))
    return totals


def pieces_of(value, count):
    parts = []
    for _ in range(count - 1):
        part = value.astype(BF16).astype(F32)
        parts.append(part)
        value = value - part
    parts.append(value)
    return parts


def split_pair(value):
    high = value.astype(BF16)
    return high, (value - high.astype(F32)).astype(BF16)


def one_hot(rows, index):
    grid = lax.broadcasted_iota(jnp.int32, (rows, index.shape[1]), 0)
    return grid == index


def as_bf16(mask):
    return jnp.where(mask, 1.0, 0.0).astype(BF16)


def peers_of(axis, count):
    me = lax.axis_index(axis)
    return me, [lax.rem(me + step, count) for step in range(1, count)]


def greet(groups):
    barrier = pltpu.get_barrier_semaphore()
    for axis, partners in groups:
        for partner in partners:
            pl.semaphore_signal(
                barrier, inc=1, device_id={axis: partner}, device_id_type=pl.DeviceIdType.MESH
            )
    pl.semaphore_wait(barrier, sum(len(partners) for _, partners in groups))


def push(axis, partner, source, target, send_sem, recv_sem):
    return pltpu.make_async_remote_copy(
        src_ref=source,
        dst_ref=target,
        send_sem=send_sem,
        recv_sem=recv_sem,
        device_id={axis: partner},
        device_id_type=pl.DeviceIdType.MESH,
    )


def project_kernel(centre, cam_ref, par_ref, table_ref, gate_ref):
    camera = camera_of(cam_ref, lax.axis_index("cam"))
    groups = par_ref.shape[1]
    source = [par_ref[k] for k in range(10)]
    feats = geometry(camera, centre, source)
    feats.append(1.0 / (1.0 + jnp.exp(-par_ref[10])))
    for channel, total in enumerate(colour_totals(camera, source[0:3], par_ref)):
        feats.append(jnp.maximum(0.0, total))
        gate_ref[channel] = jnp.where(total > 0.0, 1.0, jnp.where(total == 0.0, 0.5, 0.0))
    for f in range(FEATS):
        for piece, value in enumerate(pieces_of(feats[f], 3)):
            table_ref[pl.ds((f * 3 + piece) * groups, groups), :] = value.astype(BF16)


def send_kernel(shards, table, rows_ref, out_ref, staged, landed, send_sem, recv_sem):
    me, partners = peers_of("shard", shards)
    greet([("shard", partners)])
    groups = table.shape[0] // (3 * FEATS)
    cap = out_ref.shape[2]

    def gathered(r):
        index = rows_ref[pl.ds(r, 1), :]
        low = as_bf16(one_hot(LANES, index & (LANES - 1)))
        high = one_hot(groups, lax.shift_right_logical(index, 7))
        found = jnp.dot(table[...], low, preferred_element_type=F32)
        values = []
        for f in range(FEATS):
            base = f * 3 * groups
            value = (
                found[base : base + groups]
                + found[base + groups : base + 2 * groups]
                + found[base + 2 * groups : base + 3 * groups]
            )
            values.append(jnp.sum(jnp.where(high, value, 0.0), axis=0, keepdims=True))
        return stack_rows(values, ROWS)

    copies = []
    for step, partner in enumerate(partners):
        staged[step] = gathered(partner)
        copy = push(
            "shard",
            partner,
            staged.at[step],
            landed.at[step],
            send_sem.at[step],
            recv_sem.at[step],
        )
        copy.start()
        copies.append(copy)
    out_ref[me] = gathered(me)
    for step, copy in enumerate(copies):
        copy.wait_recv()
        out_ref[lax.rem(me + (shards - 1 - step), shards)] = landed[step]
    for copy in copies:
        copy.wait_send()


def stack_rows(values, rows):
    row = lax.broadcasted_iota(jnp.int32, (rows, values[0].shape[1]), 0)
    out = jnp.zeros(row.shape, F32)
    for k, value in enumerate(values):
        out = jnp.where(row == k, value, out)
    return out


def mono_value(kind, x, y):
    return jnp.where(
        kind == 0,
        1.0,
        jnp.where(
            kind == 1,
            x,
            jnp.where(
                kind == 2,
                y,
                jnp.where(
                    kind == 3,
                    x * x,
                    jnp.where(kind == 4, x * y, jnp.where(kind == 5, y * y, 0.0)),
                ),
            ),
        ),
    )


def pixel_offset(index):
    return (index & 15).astype(F32) - 7.5, lax.shift_right_logical(index, 4).astype(F32) - 7.5


def widen(value):
    return jnp.concatenate([value] * (BLOCK // LANES), axis=1)


def render_kernel(
    tiles,
    blocks,
    ids_ref,
    counts_ref,
    feats_ref,
    lists_ref,
    wanted_ref,
    image_ref,
    grad_ref,
    table,
    mono_row,
    upper,
    lower,
    keep_x,
    keep_wh,
    keep_wl,
    keep_f,
    carry,
    image,
    acc,
):
    shards, _, cap = feats_ref.shape
    per = cap // LANES
    groups = shards * per
    for h in range(groups):
        s, part = h // per, h % per
        block = feats_ref[s, :, part * LANES : (part + 1) * LANES]
        table[pl.ds(h * 48, 48), :] = jnp.concatenate(pieces_of(block, 3), axis=0).astype(BF16)
    k = lax.broadcasted_iota(jnp.int32, (ROWS, PIX), 0)
    x, y = pixel_offset(lax.broadcasted_iota(jnp.int32, (ROWS, PIX), 1))
    mono_row[...] = mono_value(k, x, y).astype(BF16)
    n = lax.broadcasted_iota(jnp.int32, (BLOCK, BLOCK + LANES), 0)
    m = lax.broadcasted_iota(jnp.int32, (BLOCK, BLOCK + LANES), 1)
    upper[...] = as_bf16((n < m) | (m >= BLOCK))
    lower[...] = as_bf16((n > m) | (m >= BLOCK))
    acc[...] = jnp.zeros_like(acc)
    lane = lax.broadcasted_iota(jnp.int32, (1, BLOCK), 1)

    def one_tile(t, _):
        count = counts_ref[0, t]
        grid_id = ids_ref[0, t]
        origin_x = (16 * lax.rem(grid_id, TILE_COLS) + 8).astype(F32)
        origin_y = (16 * lax.div(grid_id, TILE_COLS) + 8).astype(F32)
        steps = lax.div(count + (BLOCK - 1), BLOCK)
        carry[...] = jnp.zeros_like(carry)
        image[...] = jnp.zeros_like(image)

        def entry_index(j):
            return lists_ref[pl.ds(t * blocks + j, 1), :]

        def forward(j, _):
            index = entry_index(j)
            low = as_bf16(one_hot(LANES, index & (LANES - 1)))
            high = lax.shift_right_logical(index, 7)
            found = jnp.dot(table[...], low, preferred_element_type=F32)
            total = jnp.zeros((48, BLOCK), F32)
            for h in range(groups):
                total = total + jnp.where(high == h, found[h * 48 : (h + 1) * 48], 0.0)
            feats = total[0:16] + total[16:32] + total[32:48]
            keep_f[j] = feats
            ux = feats[0:1] - origin_x
            uy = feats[1:2] - origin_y
            c0, c1, c2 = feats[2:3], feats[3:4], feats[4:5]
            valid = j * BLOCK + lane < count
            offset = lax.broadcasted_iota(jnp.int32, (16, BLOCK), 0).astype(F32) - 7.5
            dx = offset - ux
            dy = offset - uy
            along_x = jnp.where(valid, -0.5 * c0 * dx * dx, 0.0)
            cross = jnp.where(valid, -c1 * dx, 0.0)
            along_y = jnp.where(valid, -0.5 * c2 * dy * dy, -1e30)
            value = feats[5:6] * jnp.exp(
                jnp.concatenate(
                    [
                        (along_x + along_y[r : r + 1]) + cross * dy[r : r + 1]
                        for r in range(PIX // 16)
                    ],
                    axis=0,
                )
            )
            keep_x[j] = value
            alpha = jnp.minimum(CLAMP, value)
            log_high, log_low = split_pair(jnp.log(1.0 - alpha))
            before = jnp.dot(log_high, upper[...], preferred_element_type=F32) + jnp.dot(
                log_low, upper[...], preferred_element_type=F32
            )
            held = carry[...]
            weight = alpha * jnp.exp(before[:, :BLOCK] + widen(held))
            carry[...] = held + before[:, BLOCK:]
            w_high, w_low = split_pair(weight)
            keep_wh[j] = w_high
            keep_wl[j] = w_low
            colour = stack_rows([feats[6:7], feats[7:8], feats[8:9]], 8)
            colour = jnp.concatenate(pieces_of(colour, 2), axis=0).astype(BF16)
            drawn = lax.dot_general(colour, w_high, NT, preferred_element_type=F32)
            drawn = drawn + lax.dot_general(colour, w_low, NT, preferred_element_type=F32)
            image[...] += drawn[0:8] + drawn[8:16]
            return 0

        lax.fori_loop(0, steps, forward, 0)
        shown = image[0:3]
        image_ref[t] = shown
        slope = (shown - wanted_ref[t]) * (1.0 / PIX)
        slope = stack_rows([slope[0:1], slope[1:2], slope[2:3]], 8)
        g_high, g_low = pieces_of(slope, 2)
        g_row = jnp.concatenate([g_high, g_low], axis=0).astype(BF16)
        g_col = jnp.transpose(jnp.concatenate([g_high, g_high, g_low, g_low], axis=0)).astype(BF16)
        carry[...] = jnp.zeros_like(carry)

        def backward(step, _):
            j = steps - 1 - step
            feats = keep_f[j]
            colour = stack_rows([feats[6:7], feats[7:8], feats[8:9]], 8)
            c_high, c_low = pieces_of(colour, 2)
            colour = jnp.concatenate([c_high, c_low, c_high, c_low], axis=0).astype(BF16)
            pull = jnp.dot(g_col, colour, preferred_element_type=F32)
            w_high, w_low = keep_wh[j], keep_wl[j]
            share = (w_high.astype(F32) + w_low.astype(F32)) * pull
            s_high, s_low = split_pair(share)
            after = jnp.dot(s_high, lower[...], preferred_element_type=F32) + jnp.dot(
                s_low, lower[...], preferred_element_type=F32
            )
            held = carry[...]
            behind = after[:, :BLOCK] + widen(held)
            carry[...] = held + after[:, BLOCK:]
            value = keep_x[j]
            free = value < CLAMP
            odds = value / (1.0 - jnp.minimum(value, CLAMP))
            p_high, p_low = split_pair(jnp.where(free, share - odds * behind, 0.0))
            mom = jnp.dot(mono_row[...], p_high, preferred_element_type=F32) + jnp.dot(
                mono_row[...], p_low, preferred_element_type=F32
            )
            tint = jnp.dot(g_row, w_high, preferred_element_type=F32) + jnp.dot(
                g_row, w_low, preferred_element_type=F32
            )
            tint = tint[0:8] + tint[8:16]
            ux = feats[0:1] - origin_x
            uy = feats[1:2] - origin_y
            c0, c1, c2 = feats[2:3], feats[3:4], feats[4:5]
            m0, mx, my = mom[0:1], mom[1:2], mom[2:3]
            px = mx - ux * m0
            py = my - uy * m0
            pxx = mom[3:4] - ux * (mx + px)
            pxy = mom[4:5] - ux * my - uy * px
            pyy = mom[5:6] - uy * (my + py)
            grads = stack_rows(
                [
                    c0 * px + c1 * py,
                    c2 * py + c1 * px,
                    -0.5 * pxx,
                    -pxy,
                    -0.5 * pyy,
                    m0,
                    tint[0:1],
                    tint[1:2],
                    tint[2:3],
                ],
                ROWS,
            )
            grads = jnp.concatenate(pieces_of(grads, 2), axis=0)
            index = entry_index(j)
            low = as_bf16(one_hot(LANES, index & (LANES - 1)))
            high = lax.shift_right_logical(index, 7)
            valid = j * BLOCK + lane < count
            grads = jnp.where(valid, grads, 0.0)
            spread = jnp.concatenate(
                [jnp.where(high == h, grads, 0.0) for h in range(groups)], axis=0
            ).astype(BF16)
            acc[...] += lax.dot_general(spread, low, NT, preferred_element_type=F32)
            return 0

        lax.fori_loop(0, steps, backward, 0)
        return 0

    lax.fori_loop(0, tiles, one_tile, 0)
    for h in range(groups):
        s, part = h // per, h % per
        grad_ref[s, :, part * LANES : (part + 1) * LANES] = (
            acc[pl.ds(h * 32, 16), :] + acc[pl.ds(h * 32 + 16, 16), :]
        )


def return_kernel(
    shards,
    cams,
    centre,
    cam_ref,
    par_ref,
    slot_ref,
    rows_ref,
    gate_ref,
    out_ref,
    acc,
    landed,
    mine,
    other,
    shard_send,
    shard_recv,
    cam_send,
    cam_recv,
):
    me, partners = peers_of("shard", shards)
    here, views = peers_of("cam", cams)
    greet([("shard", partners), ("cam", views)])
    size = out_ref.shape[1]
    groups = cams * size
    copies = []
    for step, partner in enumerate(partners):
        copy = push(
            "shard",
            partner,
            slot_ref.at[partner],
            landed.at[step],
            shard_send.at[step],
            shard_recv.at[step],
        )
        copy.start()
        copies.append(copy)

    def scattered(r, value):
        index = rows_ref[pl.ds(r, 1), :]
        low = as_bf16(one_hot(LANES, index & (LANES - 1)))
        high = one_hot(groups, lax.shift_right_logical(index, 7))
        parts = pieces_of(value, 2)
        spread = jnp.concatenate(
            [
                jnp.where(high, part[f : f + 1], 0.0).astype(BF16)
                for f in range(FEATS)
                for part in parts
            ],
            axis=0,
        )
        return lax.dot_general(spread, low, NT, preferred_element_type=F32)

    acc[...] = scattered(me, slot_ref[me])
    for step, copy in enumerate(copies):
        copy.wait_recv()
        acc[...] += scattered(lax.rem(me + (shards - 1 - step), shards), landed[step])
    for f in range(FEATS):
        value = acc[pl.ds(2 * f * groups, groups), :] + acc[pl.ds((2 * f + 1) * groups, groups), :]
        if f >= 6:
            value = value * gate_ref[f - 6]
        for c in range(cams):
            mine[c, f] = value[c * size : (c + 1) * size]
    swaps = []
    for step, view in enumerate(views):
        copy = push(
            "cam", view, mine.at[view], other.at[step], cam_send.at[step], cam_recv.at[step]
        )
        copy.start()
        swaps.append(copy)
    source = [par_ref[k] for k in range(10)]
    keep = 1.0 / (1.0 + jnp.exp(par_ref[10]))

    def one_view(view, feature_grad, first):
        camera = camera_of(cam_ref, view)
        _, pull_geometry = jax.vjp(lambda *s: geometry(camera, centre, s), *source)
        head = list(pull_geometry([feature_grad(f) for f in range(5)]))
        basis, pull_basis = jax.vjp(lambda *w: basis_of(camera, w), *source[0:3])
        tints = [feature_grad(6 + channel) for channel in range(3)]
        cotangent = [
            sum(tints[channel] * par_ref[11 + 16 * channel + k] for channel in range(3))
            for k in range(16)
        ]
        for k, value in enumerate(pull_basis(cotangent)):
            head[k] = head[k] + value

        def put(k, value):
            if first:
                out_ref[k] = value
            else:
                out_ref[k] += value

        for k in range(10):
            put(k, head[k])
        put(10, keep * feature_grad(5))
        for channel in range(3):
            for k in range(16):
                put(11 + 16 * channel + k, tints[channel] * basis[k])

    one_view(here, lambda f: mine[here, f], True)
    for step, copy in enumerate(swaps):
        copy.wait_recv()
        one_view(
            lax.rem(here + (cams - 1 - step), cams), lambda f, step=step: other[step, f], False
        )
    for copy in copies + swaps:
        copy.wait_send()


def local_params():
    return pltpu.CompilerParams(vmem_limit_bytes=VMEM_LIMIT)


def remote_params(number):
    return pltpu.CompilerParams(
        vmem_limit_bytes=VMEM_LIMIT, collective_id=number, has_side_effects=True
    )


VM = pl.BlockSpec(memory_space=pltpu.VMEM)
SM = pl.BlockSpec(memory_space=pltpu.SMEM)


def per_device(params, cameras, send_rows, tile_ids, tile_counts, tile_lists, targets):
    shards = lax.axis_size("shard")
    cams = lax.axis_size("cam")
    tiles, length = tile_lists.shape[1:]
    blocks = length // BLOCK
    centre = (8.0 * TILE_COLS, 8.0 * (shards * tiles // TILE_COLS))
    slots = send_rows.shape[2]
    cap = slots // shards
    groups = params.shape[1] // LANES
    size = groups // cams
    wide = params.reshape(params.shape[0], groups, LANES)
    rows = send_rows.reshape(shards, cap)
    table, gates = pl.pallas_call(
        functools.partial(project_kernel, centre),
        out_shape=(
            jax.ShapeDtypeStruct((3 * FEATS * groups, LANES), BF16),
            jax.ShapeDtypeStruct((3, groups, LANES), F32),
        ),
        in_specs=[SM, VM],
        out_specs=(VM, VM),
        compiler_params=local_params(),
        name="project",
    )(cameras, wide)
    links = pltpu.SemaphoreType.DMA((shards - 1,))
    arrived = pl.pallas_call(
        functools.partial(send_kernel, shards),
        out_shape=jax.ShapeDtypeStruct((shards, ROWS, cap), F32),
        in_specs=[VM, VM],
        out_specs=VM,
        scratch_shapes=[
            pltpu.VMEM((shards - 1, ROWS, cap), F32),
            pltpu.VMEM((shards - 1, ROWS, cap), F32),
            links,
            links,
        ],
        compiler_params=remote_params(0),
        name="send",
    )(table, rows)
    image, slot_grad = pl.pallas_call(
        functools.partial(render_kernel, tiles, blocks),
        out_shape=(
            jax.ShapeDtypeStruct((tiles, 3, PIX), F32),
            jax.ShapeDtypeStruct((shards, ROWS, cap), F32),
        ),
        in_specs=[SM, SM, VM, VM, VM],
        out_specs=(VM, VM),
        scratch_shapes=[
            pltpu.VMEM((slots // LANES * 48, LANES), BF16),
            pltpu.VMEM((ROWS, PIX), BF16),
            pltpu.VMEM((BLOCK, BLOCK + LANES), BF16),
            pltpu.VMEM((BLOCK, BLOCK + LANES), BF16),
            pltpu.VMEM((blocks, PIX, BLOCK), F32),
            pltpu.VMEM((blocks, PIX, BLOCK), BF16),
            pltpu.VMEM((blocks, PIX, BLOCK), BF16),
            pltpu.VMEM((blocks, ROWS, BLOCK), F32),
            pltpu.VMEM((PIX, LANES), F32),
            pltpu.VMEM((8, PIX), F32),
            pltpu.VMEM((slots // LANES * 32, LANES), F32),
        ],
        compiler_params=local_params(),
        name="render",
    )(
        tile_ids,
        tile_counts,
        arrived,
        tile_lists[0].reshape(tiles * blocks, BLOCK),
        targets[0],
    )
    mine = lax.dynamic_slice_in_dim(wide, lax.axis_index("cam") * size, size, axis=1)
    grad = pl.pallas_call(
        functools.partial(return_kernel, shards, cams, centre),
        out_shape=jax.ShapeDtypeStruct((params.shape[0], size, LANES), F32),
        in_specs=[SM, VM, VM, VM, VM],
        out_specs=VM,
        scratch_shapes=[
            pltpu.VMEM((2 * FEATS * groups, LANES), F32),
            pltpu.VMEM((shards - 1, ROWS, cap), F32),
            pltpu.VMEM((cams, FEATS, size, LANES), F32),
            pltpu.VMEM((cams - 1, FEATS, size, LANES), F32),
            links,
            links,
            pltpu.SemaphoreType.DMA((cams - 1,)),
            pltpu.SemaphoreType.DMA((cams - 1,)),
        ],
        compiler_params=remote_params(1),
        name="return_pull",
    )(cameras, mine, slot_grad, rows, gates)
    return (image[None], grad.reshape(params.shape[0], size * LANES))


def solution(mesh):
    placed = (
        P(None, ("groups", "shard")),
        P("groups", None),
        P(("groups", "cam"), "shard", None),
        P(("groups", "cam"), "shard"),
        P(("groups", "cam"), "shard"),
        P(("groups", "cam"), "shard", None),
        P(("groups", "cam"), "shard", None, None),
    )
    return jax.shard_map(
        per_device,
        mesh=mesh,
        in_specs=placed,
        out_specs=(P(("groups", "cam"), "shard", None, None), P(None, ("groups", "shard", "cam"))),
        check_vma=False,
    )
```
